512 devices in a mesh: seq: 64 (over y_lo, x, z), head: 8 (over y_hi, core).
Axes of the slice: x: 4, y: 8 (y_hi: 4, y_lo: 2; y = y_hi * 2 + y_lo), z: 8, core: 2. Of those that a mesh axis runs over, the one named last changes fastest.
Arguments:
- queries: bfloat16 [8192, 3072], P(('seq', 'head')), may hold values from -30 to 30
- key_rows: bfloat16 [8192, 1024], P(('seq', 'head')), may hold values from -30 to 30
- value_rows: bfloat16 [8192, 1024], P(('seq', 'head')), may hold values from -6 to 6
- block_span: int32 [128], replicated, may hold values from 0 to 3, as said below
- attend: int32 [4, 4], replicated, may hold values from 0 to 1, as said below
- noise_level: int32 [4], replicated, may hold values from 0 to 31
- gate_table: float32 [32, 3072], replicated, may hold values from 0.25 to 2
Outputs:
- gated: bfloat16 [8192, 3072], P(('seq', 'head'))
The draws below stay inside these ranges and needn't reach their ends.
Inputs may be any that keep to these rules, and one draw needn't show every extreme that they name: `block_span`: every span of 0 to 3 owns exactly 32 blocks. attend[r][r] is 1 and attend[r][s] is 0 for s > r.
All inputs are finite; a program needn't handle non-finite values.
Results may differ from the reference program's by a relative error of at most 0.01.
Values may be sent and summed in bfloat16 or wider, within the bound.
A program may use at most 64 MiB of HBM per device.

```python
import math
import jax
import jax.numpy as jnp
from jax import lax

HEADS = 24
KV_GROUPS = 8
HD = 128
SPANS = 4
LEVELS = 32
D = 3072
KVD = 1024
GROUP = 3
TOKENS = 8192
BLOCK = 64
NBLK = 128


def draw_queries(key, part):
    key = jax.random.fold_in(key, 11)
    rows = jax.random.normal(key, (TOKENS, D), jnp.float32)
    return rows.astype(jnp.bfloat16)


def draw_key_rows(key, part):
    key = jax.random.fold_in(key, 23)
    rows = jax.random.normal(key, (TOKENS, KVD), jnp.float32)
    return rows.astype(jnp.bfloat16)


def draw_block_span(key, part):
    key = jax.random.fold_in(key, 37)
    order = jax.random.permutation(key, NBLK).astype(jnp.int32)
    return (order * SPANS // NBLK).astype(jnp.int32)


def draw_attend(key, part):
    key = jax.random.fold_in(key, 41)
    coins = jax.random.randint(key, (SPANS, SPANS), 0, 2).astype(jnp.int32)
    reader = jnp.arange(SPANS, dtype=jnp.int32)[:, None]
    source = jnp.arange(SPANS, dtype=jnp.int32)[None, :]
    below = jnp.where(source < reader, coins, 0)
    return jnp.where(source == reader, 1, below).astype(jnp.int32)


def with_ends(array, rng, low, largest):
    longest = array.shape.index(max(array.shape))
    spots = []
    for shift in (0, 1):
        where = [jax.random.randint(jax.random.fold_in(rng, axis), (), 0, length) for axis, length in enumerate(array.shape)]
        where[longest] = (where[longest] + shift) % array.shape[longest]
        spots.append(tuple(where))
    return array.at[spots[0]].set(low).at[spots[1]].set(largest)


def levels(stream_key, dims, cuts, smallest, high):
    def one(position, parts):
        heights = jax.random.uniform(jax.random.fold_in(jax.random.fold_in(stream_key, 6), position), (parts,), jnp.float32, smallest / len(cuts), high / len(cuts))
        return jnp.repeat(jnp.exp(heights), dims[position] // parts).reshape((-1,) + (1,) * (len(dims) - position - 1))

    level = one(*cuts[0])
    for cut in cuts[1:]:
        level = level * one(*cut)
    return level


def normal_values(own_key, extent, deviation, limit, pieces=(), kind=jnp.bfloat16):
    entries = jax.random.normal(own_key, extent, jnp.float32) * deviation
    if len(pieces) > 0:
        entries = levels(own_key, extent, pieces, -0.22, 0.18) * entries
    return jnp.clip(entries, min=-limit, max=limit).astype(kind)


def setup_inputs(seed: int = 0) -> dict:
    streams_of = jax.random.split(jax.random.key(seed), 8)
    queries = draw_queries(jax.random.fold_in(streams_of[7], 71), 0)
    key_rows = draw_key_rows(jax.random.fold_in(streams_of[7], 71), 0)
    value_rows = normal_values(streams_of[2], (TOKENS, KVD), 1.0, 6.0, ((0, 512),))
    block_span = draw_block_span(jax.random.fold_in(streams_of[7], 71), 0)
    attend = draw_attend(jax.random.fold_in(streams_of[7], 71), 0)
    noise_level = with_ends(jax.random.randint(streams_of[5], (SPANS,), 0, LEVELS), jax.random.fold_in(streams_of[5], 1), 0, LEVELS - 1).astype(jnp.int32)
    gate_table = jnp.clip(jnp.exp(jax.random.uniform(streams_of[6], (LEVELS, D), jnp.float32, math.log(0.25), math.log(2.0))), 0.25, 2.0)
    return dict(queries=queries, key_rows=key_rows, value_rows=value_rows, block_span=block_span, attend=attend, noise_level=noise_level, gate_table=gate_table)


def reference(queries, key_rows, value_rows, block_span, attend, noise_level, gate_table):
    positions = jnp.arange(TOKENS, dtype=jnp.int32)
    span_of_token = block_span[(positions // BLOCK).astype(jnp.int32)]
    allowed = attend[span_of_token][:, span_of_token] > 0
    head_q = jnp.moveaxis(queries.reshape(TOKENS, HEADS, HD), 1, 0)
    group_k = jnp.moveaxis(key_rows.reshape(TOKENS, KV_GROUPS, HD), 1, 0)
    group_v = jnp.moveaxis(value_rows.reshape(TOKENS, KV_GROUPS, HD), 1, 0)
    score_scale = HD ** -0.5

    def one_head(pair):
        q_part, group_index = pair
        k_part = group_k[group_index]
        v_part = group_v[group_index]
        scores = jnp.dot(q_part, k_part.T, preferred_element_type=jnp.float32) * score_scale
        masked = jnp.where(allowed, scores, -jnp.inf)
        row_top = jnp.max(masked, axis=1, keepdims=True)
        probs = jnp.where(allowed, jnp.exp(scores - row_top), 0.0)
        weights = probs.astype(jnp.bfloat16)
        summed = jnp.dot(weights, v_part, preferred_element_type=jnp.float32)
        return (summed / jnp.sum(probs, axis=1, keepdims=True)).astype(jnp.bfloat16)

    group_ids = (jnp.arange(HEADS, dtype=jnp.int32) // GROUP).astype(jnp.int32)
    attn = lax.map(one_head, (head_q, group_ids))
    attn = jnp.moveaxis(attn, 0, 1).reshape(TOKENS, D)
    level = noise_level[span_of_token]
    gate_rows = gate_table[level]
    return (gate_rows * attn.astype(jnp.float32)).astype(jnp.bfloat16)
```

```python
import functools
import math

import jax
import jax.numpy as jnp
from jax import lax
from jax.experimental import pallas as pl
from jax.experimental.pallas import tpu as pltpu
from jax.sharding import PartitionSpec as P

MESH = pl.DeviceIdType.MESH
HD = 128
NX, NY, NZ = 4, 8, 8
ROWS = 16
HPG = 3
TOK = NY * ROWS
QR = HPG * TOK
COEF = HD**-0.5 * math.log2(math.e)
NEG = -1e30

Y_FAR = (4, 3, 5, 2, 6, 1, 7)
Y_NEAR = (1, 7, 2, 6, 3, 5, 4)
Z_DIRECT = (1, 7, 2, 6, 3, 5)
X_FAR = (2, 1, 3)


def wrap(a, n):
    return lax.rem(a + n, n)


def place():
    seq, head = lax.axis_index("seq"), lax.axis_index("head")
    z, x, y_lo = lax.rem(seq, NZ), lax.rem(seq // NZ, NX), seq // (NZ * NX)
    return x, (head // 2) * 2 + y_lo, z, lax.rem(head, 2)


def device(x, y, z, core):
    return ((lax.rem(y, 2) * NX + x) * NZ + z, (y // 2) * 2 + core)


def block_of(x, y, z):
    return ((lax.rem(y, 2) * NX + x) * NZ + z) * 2 + y // 4


def kernel(
    q_hbm, k_hbm, v_hbm, span_ref, attend_ref, level_ref, gate_hbm, out_ref,
    q_in, k_in, v_in, gate, kv, qs, kaug, qaug, vt, acc, top, o_send, s_send, o_recv, s_recv,
    attn_send, attn, in_sem, ykv_s, ykv_r, yq_s, yq_r, z_s, z_r, z4_s, z4_r, c_s, c_r, xq_s, xq_r,
    xo_s, xo_r, xs_s, xs_r, yo_s, yo_r,
):
    x, y, z, core = place()

    def at_x(d):
        return device(wrap(x + d, NX), y, z, core)

    def at_y(d):
        return device(x, wrap(y + d, NY), z, core)

    def at_z(d):
        return device(x, y, wrap(z + d, NZ), core)

    sibling = device(x, y, z, 1 - core)

    def remote(src, dst, ss, rs, to):
        return pltpu.make_async_remote_copy(
            src_ref=src, dst_ref=dst, send_sem=ss, recv_sem=rs, device_id=to, device_id_type=MESH
        )

    loads = [
        pltpu.make_async_copy(k_hbm, k_in, in_sem.at[0]),
        pltpu.make_async_copy(v_hbm, v_in, in_sem.at[1]),
        pltpu.make_async_copy(q_hbm, q_in, in_sem.at[2]),
        pltpu.make_async_copy(gate_hbm, gate, in_sem.at[3]),
    ]
    for load in loads:
        load.start()
    barrier = pltpu.get_barrier_semaphore()
    peers = [at_y(d) for d in Y_FAR] + [at_z(d) for d in Z_DIRECT] + [at_x(d) for d in X_FAR]
    peers.append(sibling)
    for peer in peers:
        pl.semaphore_signal(barrier, inc=1, device_id=peer, device_id_type=MESH)

    lane = lax.broadcasted_iota(jnp.int32, (ROWS, HD), 1)
    for i in range(NY):
        ys = wrap(y - i, NY)
        for j in range(NZ):
            span = span_ref[block_of(x, ys, wrap(z - j, NZ))]
            kaug[j, i * ROWS : (i + 1) * ROWS, :] = jnp.where(lane == span, 1.0, 0.0).astype(jnp.bfloat16)
        for j in range(NX):
            span = span_ref[block_of(wrap(x - j, NX), ys, z)]
            bias = jnp.zeros((ROWS, HD), jnp.float32)
            for s in range(4):
                low = jnp.where(attend_ref[span, s] > 0, 0.0, NEG)
                bias = jnp.where(lane == s, low, bias)
            qaug[j, i * ROWS : (i + 1) * ROWS, :] = bias.astype(jnp.bfloat16)

    for load in loads:
        load.wait()
    pl.semaphore_wait(barrier, len(peers))

    def group(d):
        return wrap(y + d, NY)

    def columns(first, count):
        return pl.ds(pl.multiple_of(first * HD, HD), count * HD)

    for d in Y_FAR:
        cols = columns(group(d), 1)
        remote(k_in.at[:, cols], kv.at[0, 0, 0, d], ykv_s.at[d], ykv_r.at[d], at_y(d)).start()
        remote(v_in.at[:, cols], kv.at[0, 0, 1, d], ykv_s.at[d], ykv_r.at[d], at_y(d)).start()
    for d in Y_FAR:
        for h in range(HPG):
            remote(
                q_in.at[:, columns(group(d) * HPG + h, 1)], qs.at[0, h, d], yq_s.at[d], yq_r.at[d], at_y(d)
            ).start()
    kv[0, 0, 0, 0] = k_in[:, columns(y, 1)]
    kv[0, 0, 1, 0] = v_in[:, columns(y, 1)]
    for h in range(HPG):
        qs[0, h, 0] = q_in[:, columns(y * HPG + h, 1)]

    def send_kv(i):
        for d in Z_DIRECT:
            remote(kv.at[0, 0, :, i], kv.at[0, d, :, i], z_s.at[d], z_r.at[d], at_z(d)).start()

    def send_q(i):
        for d in X_FAR:
            remote(qs.at[0, :, i], qs.at[d, :, i], xq_s.at[d], xq_r.at[d], at_x(d)).start()

    send_kv(0)
    send_q(0)
    for d in Y_NEAR:
        unit = kv.at[0, 0, :, d]
        remote(unit, unit, ykv_s.at[d], ykv_r.at[d], sibling).wait_recv()
        send_kv(d)
    remote(kv.at[0, 0], kv.at[1, 0], c_s.at[0], c_r.at[0], sibling).start()
    for d in Y_NEAR:
        unit = qs.at[0, :, d]
        remote(unit, unit, yq_s.at[d], yq_r.at[d], sibling).wait_recv()
        send_q(d)

    def arrive(d):
        slot = kv.at[0, d]
        remote(slot, slot, z_s.at[d], z_r.at[d], sibling).wait_recv()
        remote(slot, kv.at[1, d], c_s.at[d], c_r.at[d], sibling).start()

    def from_sibling(d):
        slot = kv.at[1, d]
        remote(slot, slot, c_s.at[d], c_r.at[d], sibling).wait_recv()

    def turn_values(step, parts):
        for n, (p, d) in enumerate(parts):
            vals = kv[p, d, 1].reshape(TOK, HD)
            vt[step, :, n * TOK : (n + 1) * TOK] = vals.astype(jnp.float32).T.astype(jnp.bfloat16)

    def absorb(step, parts, b, first):
        keys = jnp.concatenate([kv[p, d, 0].reshape(TOK, HD) for p, d in parts], axis=0)
        marks = jnp.concatenate([kaug[d] for _, d in parts], axis=0)
        left = jnp.concatenate([keys, marks], axis=1)
        right = jnp.concatenate(
            [qs[b].reshape(QR, HD), jnp.concatenate([qaug[b]] * HPG, axis=0)], axis=1
        )
        scores = lax.dot_general(left, right, (((1,), (1,)), ((), ())), preferred_element_type=jnp.float32)
        high = jnp.max(scores, axis=0, keepdims=True)
        if not first:
            old = top[b]
            high = jnp.maximum(high, old)
        probs = jnp.exp2((scores - high) * COEF).astype(jnp.bfloat16)
        vals = jnp.concatenate([vt[step], jnp.ones((16, 2 * TOK), jnp.bfloat16)], axis=0)
        new = jnp.dot(vals, probs, preferred_element_type=jnp.float32)
        if first:
            acc[b] = new
        else:
            acc[b] = acc[b] * jnp.exp2((old - high) * COEF) + new
        top[b] = high

    steps = [
        ((0, 0), (1, 0)),
        ((0, 1), (0, 7)),
        ((1, 1), (1, 7)),
        ((0, 2), (0, 6)),
        ((1, 2), (1, 6)),
        ((0, 3), (0, 5)),
        ((1, 3), (1, 5)),
        ((0, 4), (1, 4)),
    ]

    from_sibling(0)
    turn_values(0, steps[0])
    absorb(0, steps[0], 0, True)
    arrive(1)
    arrive(7)
    arrive(2)
    arrive(6)
    remote(kv.at[0, 2, 0], kv.at[0, 4, 0], z4_s.at[0], z4_r.at[0], at_z(2)).start()
    remote(kv.at[0, 6, 1], kv.at[0, 4, 1], z4_s.at[1], z4_r.at[1], at_z(6)).start()
    for d in X_FAR:
        block = qs.at[d]
        remote(block, block, xq_s.at[d], xq_r.at[d], sibling).wait_recv()
    for b in (1, 2, 3):
        absorb(0, steps[0], b, True)
    arrive(3)
    arrive(5)
    for step in (1, 2, 3, 4):
        if step in (2, 4):
            for _, d in steps[step]:
                from_sibling(d)
        turn_values(step, steps[step])
        for b in range(NX):
            absorb(step, steps[step], b, False)
        if step == 2:
            for half in (0, 1):
                slot = kv.at[0, 4, half]
                remote(slot, slot, z4_s.at[half], z4_r.at[half], sibling).wait_recv()
            remote(kv.at[0, 4], kv.at[1, 4], c_s.at[4], c_r.at[4], sibling).start()
    from_sibling(3)
    from_sibling(5)
    from_sibling(4)
    for step in (5, 6, 7):
        turn_values(step, steps[step])
    for b in (2, 1, 3, 0):
        for step in (5, 6, 7):
            absorb(step, steps[step], b, False)
        if b:
            o_send[b] = (acc[b, 0:HD, :] / acc[b, HD : HD + 1, :]).astype(jnp.bfloat16)
            s_send[b] = jnp.concatenate([top[b], acc[b, HD : HD + 7, :]], axis=0)
            to = at_x(-b)
            remote(o_send.at[b], o_recv.at[b], xo_s.at[b], xo_r.at[b], to).start()
            remote(s_send.at[b], s_recv.at[b], xs_s.at[b], xs_r.at[b], to).start()

    for b in (1, 2, 3):
        part, stat = o_recv.at[b], s_recv.at[b]
        remote(stat, stat, xs_s.at[b], xs_r.at[b], sibling).wait_recv()
        remote(part, part, xo_s.at[b], xo_r.at[b], sibling).wait_recv()
    tops = [top[0]] + [s_recv[b, 0:1, :] for b in (1, 2, 3)]
    highest = functools.reduce(jnp.maximum, tops)
    scales = [jnp.exp2((t - highest) * COEF) for t in tops]
    sums = [acc[0, HD : HD + 1, :]] + [s_recv[b, 1:2, :] for b in (1, 2, 3)]
    shares = [scale * total for scale, total in zip(scales, sums)]
    whole = 1.0 / functools.reduce(jnp.add, shares)
    merged = acc[0, 0:HD, :] * (scales[0] * whole)
    for b in (1, 2, 3):
        merged = merged + o_recv[b].astype(jnp.float32) * (shares[b] * whole)
    for h in range(HPG):
        rows = merged[:, h * TOK : (h + 1) * TOK].T.astype(jnp.bfloat16)
        for i in range(NY):
            attn_send[i, :, h * HD : (h + 1) * HD] = rows[i * ROWS : (i + 1) * ROWS, :]
    for d in Y_FAR:
        remote(attn_send.at[d], attn.at[y], yo_s.at[d], yo_r.at[d], at_y(-d)).start()
    attn[y] = attn_send[0]
    level = level_ref[span_ref[block_of(x, y, z)]]
    gates = gate[pl.ds(level, 1), :]
    for d in Y_NEAR:
        unit = attn_send.at[d]
        remote(unit, unit, yo_s.at[d], yo_r.at[d], sibling).wait_recv()
    for g in range(NY):
        cols = slice(g * HPG * HD, (g + 1) * HPG * HD)
        out_ref[:, cols] = (gates[:, cols] * attn[g].astype(jnp.float32)).astype(jnp.bfloat16)

    for d in Y_NEAR:
        remote(kv.at[0, 0, :, d], kv.at[0, 0, :, d], ykv_s.at[d], ykv_r.at[d], sibling).wait_send()
        remote(qs.at[0, :, d], qs.at[0, :, d], yq_s.at[d], yq_r.at[d], sibling).wait_send()
        remote(attn_send.at[d], attn_send.at[d], yo_s.at[d], yo_r.at[d], sibling).wait_send()
    for d in Z_DIRECT:
        remote(kv.at[0, 0], kv.at[0, 0], z_s.at[d], z_r.at[d], sibling).wait_send()
    for half in (0, 1):
        remote(kv.at[0, 4, half], kv.at[0, 4, half], z4_s.at[half], z4_r.at[half], sibling).wait_send()
    for d in range(NZ):
        remote(kv.at[0, d], kv.at[0, d], c_s.at[d], c_r.at[d], sibling).wait_send()
    for d in X_FAR:
        remote(qs.at[0], qs.at[0], xq_s.at[d], xq_r.at[d], sibling).wait_send()
        remote(o_send.at[d], o_send.at[d], xo_s.at[d], xo_r.at[d], sibling).wait_send()
        remote(s_send.at[d], s_send.at[d], xs_s.at[d], xs_r.at[d], sibling).wait_send()


def local(queries, key_rows, value_rows, block_span, attend, noise_level, gate_table):
    bf16, f32 = jnp.bfloat16, jnp.float32
    dma = pltpu.SemaphoreType.DMA
    anywhere = pl.BlockSpec(memory_space=pl.ANY)
    smem = pl.BlockSpec(memory_space=pltpu.SMEM)
    return pl.pallas_call(
        kernel,
        out_shape=jax.ShapeDtypeStruct(queries.shape, bf16),
        in_specs=[anywhere, anywhere, anywhere, smem, smem, smem, anywhere],
        out_specs=pl.BlockSpec(memory_space=pltpu.VMEM),
        scratch_shapes=[
            pltpu.VMEM(queries.shape, bf16),
            pltpu.VMEM(key_rows.shape, bf16),
            pltpu.VMEM(value_rows.shape, bf16),
            pltpu.VMEM(gate_table.shape, f32),
            pltpu.VMEM((2, NZ, 2, NY, ROWS, HD), bf16),
            pltpu.VMEM((NX, HPG, NY, ROWS, HD), bf16),
            pltpu.VMEM((NZ, TOK, HD), bf16),
            pltpu.VMEM((NX, TOK, HD), bf16),
            pltpu.VMEM((8, HD, 2 * TOK), bf16),
            pltpu.VMEM((NX, HD + 16, QR), f32),
            pltpu.VMEM((NX, 1, QR), f32),
            pltpu.VMEM((NX, HD, QR), bf16),
            pltpu.VMEM((NX, 8, QR), f32),
            pltpu.VMEM((NX, HD, QR), bf16),
            pltpu.VMEM((NX, 8, QR), f32),
            pltpu.VMEM((NY, ROWS, HPG * HD), bf16),
            pltpu.VMEM((NY, ROWS, HPG * HD), bf16),
            dma((4,)),
            dma((8,)), dma((8,)), dma((8,)), dma((8,)),
            dma((8,)), dma((8,)), dma((2,)), dma((2,)),
            dma((8,)), dma((8,)),
            dma((4,)), dma((4,)), dma((4,)), dma((4,)), dma((4,)), dma((4,)),
            dma((8,)), dma((8,)),
        ],
        compiler_params=pltpu.CompilerParams(
            collective_id=0, has_side_effects=True, vmem_limit_bytes=48 << 20
        ),
    )(queries, key_rows, value_rows, block_span, attend, noise_level, gate_table)


def solution(mesh):
    rows = P(("seq", "head"), None)
    return jax.shard_map(
        local,
        mesh=mesh,
        in_specs=(rows, rows, rows, P(), P(), P(), P()),
        out_specs=rows,
        check_vma=False,
    )
```

```python
import functools
import math

import jax
import jax.numpy as jnp
from jax import lax
from jax.experimental import pallas as pl
from jax.experimental.pallas import tpu as pltpu
from jax.sharding import PartitionSpec as P

MESH = pl.DeviceIdType.MESH
HD = 128
NX, NY, NZ = 4, 8, 8
ROWS = 16
HPG = 3
TOK = NY * ROWS
QR = HPG * TOK
COEF = HD**-0.5 * math.log2(math.e)
NEG = -1e30

Y_FAR = (4, 3, 5, 2, 6, 1, 7)
Y_NEAR = (1, 7, 2, 6, 3, 5, 4)
Z_DIRECT = (2, 6, 1, 7)
X_FAR = (2, 1, 3)


def wrap(a, n):
    return lax.rem(a + n, n)


def place():
    seq, head = lax.axis_index("seq"), lax.axis_index("head")
    z, x, y_lo = lax.rem(seq, NZ), lax.rem(seq // NZ, NX), seq // (NZ * NX)
    return x, (head // 2) * 2 + y_lo, z, lax.rem(head, 2)


def device(x, y, z, core):
    return ((lax.rem(y, 2) * NX + x) * NZ + z, (y // 2) * 2 + core)


def block_of(x, y, z):
    return ((lax.rem(y, 2) * NX + x) * NZ + z) * 2 + y // 4


def kernel(
    q_hbm, k_hbm, v_hbm, span_hbm, attend_hbm, level_hbm, gate_hbm, out_ref,
    q_in, k_in, v_in, gate, span_ref, attend_ref, level_ref, kv, qs, kaug, qaug, vt, acc, top, o_send, s_send, o_recv, s_recv,
    attn_send, attn, in_sem, ykv_s, ykv_r, yq_s, yq_r, z_s, z_r, zu_r, z4_s, z4_r, c_s, c_r, xq_s, xq_r,
    xo_s, xo_r, xs_s, xs_r, yo_s, yo_r,
):
    x, y, z, core = place()

    def at_x(d):
        return device(wrap(x + d, NX), y, z, core)

    def at_y(d):
        return device(x, wrap(y + d, NY), z, core)

    def at_z(d):
        return device(x, y, wrap(z + d, NZ), core)

    sibling = device(x, y, z, 1 - core)

    def remote(src, dst, ss, rs, to):
        return pltpu.make_async_remote_copy(
            src_ref=src, dst_ref=dst, send_sem=ss, recv_sem=rs, device_id=to, device_id_type=MESH
        )

    small = [
        pltpu.make_async_copy(span_hbm, span_ref, in_sem.at[4]),
        pltpu.make_async_copy(attend_hbm, attend_ref, in_sem.at[5]),
        pltpu.make_async_copy(level_hbm, level_ref, in_sem.at[6]),
    ]
    loads = [
        pltpu.make_async_copy(k_hbm, k_in, in_sem.at[0]),
        pltpu.make_async_copy(v_hbm, v_in, in_sem.at[1]),
        pltpu.make_async_copy(q_hbm, q_in, in_sem.at[2]),
        pltpu.make_async_copy(gate_hbm, gate, in_sem.at[3]),
    ]
    for load in small + loads:
        load.start()
    barrier = pltpu.get_barrier_semaphore()
    peers = [at_y(d) for d in Y_FAR] + [at_z(d) for d in Z_DIRECT] + [at_x(d) for d in X_FAR]
    peers.append(sibling)
    for peer in peers:
        pl.semaphore_signal(barrier, inc=1, device_id=peer, device_id_type=MESH)

    for load in small:
        load.wait()

    lane = lax.broadcasted_iota(jnp.int32, (ROWS, HD), 1)
    for i in range(NY):
        ys = wrap(y - i, NY)
        for j in range(NZ):
            span = span_ref[block_of(x, ys, wrap(z - j, NZ))]
            kaug[j, i * ROWS : (i + 1) * ROWS, :] = jnp.where(lane == span, 1.0, 0.0).astype(jnp.bfloat16)
        for j in range(NX):
            span = span_ref[block_of(wrap(x - j, NX), ys, z)]
            bias = jnp.zeros((ROWS, HD), jnp.float32)
            for s in range(4):
                low = jnp.where(attend_ref[span, s] > 0, 0.0, NEG)
                bias = jnp.where(lane == s, low, bias)
            qaug[j, i * ROWS : (i + 1) * ROWS, :] = bias.astype(jnp.bfloat16)

    for load in loads:
        load.wait()
    pl.semaphore_wait(barrier, len(peers))

    def group(d):
        return wrap(y + d, NY)

    def columns(first, count):
        return pl.ds(pl.multiple_of(first * HD, HD), count * HD)

    for d in Y_FAR:
        cols = columns(group(d), 1)
        remote(k_in.at[:, cols], kv.at[0, 0, 0, d], ykv_s.at[d], ykv_r.at[d], at_y(d)).start()
        remote(v_in.at[:, cols], kv.at[0, 0, 1, d], ykv_s.at[d], ykv_r.at[d], at_y(d)).start()
    for d in Y_FAR:
        for h in range(HPG):
            remote(
                q_in.at[:, columns(group(d) * HPG + h, 1)], qs.at[0, h, d], yq_s.at[d], yq_r.at[d], at_y(d)
            ).start()
    kv[0, 0, 0, 0] = k_in[:, columns(y, 1)]
    kv[0, 0, 1, 0] = v_in[:, columns(y, 1)]
    for h in range(HPG):
        qs[0, h, 0] = q_in[:, columns(y * HPG + h, 1)]

    def send_kv(i):
        unit = kv.at[0, 0, :, i]
        for d in Z_DIRECT:
            got = zu_r.at[d // 4, i] if d in (2, 6) else z_r.at[d]
            remote(unit, kv.at[0, d, :, i], z_s.at[d], got, at_z(d)).start()
        remote(unit, kv.at[1, 0, :, i], c_s.at[0], c_r.at[0], sibling).start()

    def send_q(i):
        for d in X_FAR:
            remote(qs.at[0, :, i], qs.at[d, :, i], xq_s.at[d], xq_r.at[d], at_x(d)).start()

    def take_kv(d):
        unit = kv.at[0, 0, :, d]
        remote(unit, unit, ykv_s.at[d], ykv_r.at[d], sibling).wait_recv()
        send_kv(d)

    def take_q(d):
        unit = qs.at[0, :, d]
        remote(unit, unit, yq_s.at[d], yq_r.at[d], sibling).wait_recv()
        send_q(d)

    def relay(i):
        for side, d, third, hop in ((0, 2, 3, 1), (1, 6, 5, 7)):
            unit, half = kv.at[0, d, :, i], kv.at[0, d, side, i]
            remote(unit, unit, z_s.at[d], zu_r.at[side, i], sibling).wait_recv()
            remote(unit, kv.at[0, third, :, i], z_s.at[third], z_r.at[third], at_z(hop)).start()
            remote(half, kv.at[0, 4, side, i], z4_s.at[side], z4_r.at[side], at_z(d)).start()
            remote(unit, kv.at[1, d, :, i], c_s.at[d], c_r.at[d], sibling).start()

    def share(d):
        remote(kv.at[0, d], kv.at[1, d], c_s.at[d], c_r.at[d], sibling).start()

    def arrive(d):
        slot = kv.at[0, d]
        remote(slot, slot, z_s.at[d], z_r.at[d], sibling).wait_recv()
        share(d)

    def from_sibling(d):
        slot = kv.at[1, d]
        remote(slot, slot, c_s.at[d], c_r.at[d], sibling).wait_recv()

    def take_block(d):
        block = qs.at[d]
        remote(block, block, xq_s.at[d], xq_r.at[d], sibling).wait_recv()

    def turn_values(first, parts):
        for n, (p, d) in enumerate(parts):
            vals = kv[p, d, 1].reshape(TOK, HD)
            vt[:, (first + n) * TOK : (first + n + 1) * TOK] = vals.astype(jnp.float32).T.astype(jnp.bfloat16)

    def absorb(first, parts, blocks, done=lambda b: None):
        keys = jnp.concatenate([kv[p, d, 0].reshape(TOK, HD) for p, d in parts], axis=0)
        marks = jnp.concatenate([kaug[d] for _, d in parts], axis=0)
        left = jnp.concatenate([keys, marks], axis=1)
        count = len(parts) * TOK
        vals = jnp.concatenate(
            [vt[:, first * TOK : first * TOK + count], jnp.ones((16, count), jnp.bfloat16)], axis=0
        )

        def score(b):
            right = jnp.concatenate(
                [qs[b].reshape(QR, HD), jnp.concatenate([qaug[b]] * HPG, axis=0)], axis=1
            )
            return lax.dot_general(left, right, (((1,), (1,)), ((), ())), preferred_element_type=jnp.float32)

        ahead = score(blocks[0])
        for n, b in enumerate(blocks):
            scores = ahead
            if n + 1 < len(blocks):
                ahead = score(blocks[n + 1])
            high = jnp.max(scores, axis=0, keepdims=True)
            if first:
                old = top[b]
                high = jnp.maximum(high, old)
            probs = jnp.exp2((scores - high) * COEF).astype(jnp.bfloat16)
            new = jnp.dot(vals, probs, preferred_element_type=jnp.float32)
            acc[b] = acc[b] * jnp.exp2((old - high) * COEF) + new if first else new
            top[b] = high
            done(b)

    near = [(0, 0), (1, 0), (0, 1), (0, 7), (1, 1), (1, 7), (0, 2), (0, 6), (1, 2), (1, 6)]
    far = [(0, 3), (0, 5), (1, 3), (1, 5), (0, 4), (1, 4)]

    send_kv(0)
    send_q(0)
    for d in (1, 7, 2, 6):
        take_kv(d)
    relay(0)
    for d in (3, 5, 4):
        take_kv(d)
    for d in Y_NEAR:
        take_q(d)
    for d in Y_NEAR:
        relay(d)
    arrive(1)
    arrive(7)
    for d in (0, 2, 6, 1, 7):
        from_sibling(d)
    turn_values(0, near)
    absorb(0, near, [0])
    take_block(1)
    take_block(3)
    absorb(0, near, [1, 3])
    arrive(3)
    arrive(5)
    take_block(2)
    absorb(0, near, [2])
    for half in (0, 1):
        slot = kv.at[0, 4, half]
        remote(slot, slot, z4_s.at[half], z4_r.at[half], sibling).wait_recv()
    share(4)
    for d in (3, 5, 4):
        from_sibling(d)
    turn_values(len(near), far)

    def give(b):
        if b:
            o_send[b] = (acc[b, 0:HD, :] / acc[b, HD : HD + 1, :]).astype(jnp.bfloat16)
            s_send[b] = jnp.concatenate([top[b], acc[b, HD : HD + 7, :]], axis=0)
            to = at_x(-b)
            remote(o_send.at[b], o_recv.at[b], xo_s.at[b], xo_r.at[b], to).start()
            remote(s_send.at[b], s_recv.at[b], xs_s.at[b], xs_r.at[b], to).start()

    absorb(len(near), far, [2, 1, 3, 0], give)

    for b in (1, 2, 3):
        part, stat = o_recv.at[b], s_recv.at[b]
        remote(stat, stat, xs_s.at[b], xs_r.at[b], sibling).wait_recv()
        remote(part, part, xo_s.at[b], xo_r.at[b], sibling).wait_recv()
    tops = [top[0]] + [s_recv[b, 0:1, :] for b in (1, 2, 3)]
    highest = functools.reduce(jnp.maximum, tops)
    scales = [jnp.exp2((t - highest) * COEF) for t in tops]
    sums = [acc[0, HD : HD + 1, :]] + [s_recv[b, 1:2, :] for b in (1, 2, 3)]
    shares = [scale * total for scale, total in zip(scales, sums)]
    whole = 1.0 / functools.reduce(jnp.add, shares)
    merged = acc[0, 0:HD, :] * (scales[0] * whole)
    for b in (1, 2, 3):
        merged = merged + o_recv[b].astype(jnp.float32) * (shares[b] * whole)
    for h in range(HPG):
        rows = merged[:, h * TOK : (h + 1) * TOK].T.astype(jnp.bfloat16)
        for i in range(NY):
            attn_send[i, :, h * HD : (h + 1) * HD] = rows[i * ROWS : (i + 1) * ROWS, :]
    for d in Y_FAR:
        remote(attn_send.at[d], attn.at[y], yo_s.at[d], yo_r.at[d], at_y(-d)).start()
    attn[y] = attn_send[0]
    level = level_ref[span_ref[block_of(x, y, z)]]
    gates = gate[pl.ds(level, 1), :]
    for d in Y_NEAR:
        unit = attn_send.at[d]
        remote(unit, unit, yo_s.at[d], yo_r.at[d], sibling).wait_recv()
    for g in range(NY):
        cols = slice(g * HPG * HD, (g + 1) * HPG * HD)
        out_ref[:, cols] = (gates[:, cols] * attn[g].astype(jnp.float32)).astype(jnp.bfloat16)

    for d in Y_NEAR:
        remote(kv.at[0, 0, :, d], kv.at[0, 0, :, d], ykv_s.at[d], ykv_r.at[d], sibling).wait_send()
        remote(qs.at[0, :, d], qs.at[0, :, d], yq_s.at[d], yq_r.at[d], sibling).wait_send()
        remote(attn_send.at[d], attn_send.at[d], yo_s.at[d], yo_r.at[d], sibling).wait_send()
    for d in Z_DIRECT + (3, 5):
        remote(kv.at[0, 0], kv.at[0, 0], z_s.at[d], z_r.at[d], sibling).wait_send()
    for half in (0, 1):
        remote(kv.at[0, 4, half], kv.at[0, 4, half], z4_s.at[half], z4_r.at[half], sibling).wait_send()
    for d in range(NZ):
        remote(kv.at[0, d], kv.at[0, d], c_s.at[d], c_r.at[d], sibling).wait_send()
    for d in X_FAR:
        remote(qs.at[0], qs.at[0], xq_s.at[d], xq_r.at[d], sibling).wait_send()
        remote(o_send.at[d], o_send.at[d], xo_s.at[d], xo_r.at[d], sibling).wait_send()
        remote(s_send.at[d], s_send.at[d], xs_s.at[d], xs_r.at[d], sibling).wait_send()


def local(queries, key_rows, value_rows, block_span, attend, noise_level, gate_table):
    bf16, f32 = jnp.bfloat16, jnp.float32
    dma = pltpu.SemaphoreType.DMA
    hbm = pl.BlockSpec(memory_space=pltpu.HBM)
    return pl.pallas_call(
        kernel,
        out_shape=jax.ShapeDtypeStruct(queries.shape, bf16),
        in_specs=[hbm] * 7,
        out_specs=pl.BlockSpec(memory_space=pltpu.VMEM),
        scratch_shapes=[
            pltpu.VMEM(queries.shape, bf16),
            pltpu.VMEM(key_rows.shape, bf16),
            pltpu.VMEM(value_rows.shape, bf16),
            pltpu.VMEM(gate_table.shape, f32),
            pltpu.SMEM(block_span.shape, jnp.int32),
            pltpu.SMEM(attend.shape, jnp.int32),
            pltpu.SMEM(noise_level.shape, jnp.int32),
            pltpu.VMEM((2, NZ, 2, NY, ROWS, HD), bf16),
            pltpu.VMEM((NX, HPG, NY, ROWS, HD), bf16),
            pltpu.VMEM((NZ, TOK, HD), bf16),
            pltpu.VMEM((NX, TOK, HD), bf16),
            pltpu.VMEM((HD, 2 * NZ * TOK), bf16),
            pltpu.VMEM((NX, HD + 16, QR), f32),
            pltpu.VMEM((NX, 1, QR), f32),
            pltpu.VMEM((NX, HD, QR), bf16),
            pltpu.VMEM((NX, 8, QR), f32),
            pltpu.VMEM((NX, HD, QR), bf16),
            pltpu.VMEM((NX, 8, QR), f32),
            pltpu.VMEM((NY, ROWS, HPG * HD), bf16),
            pltpu.VMEM((NY, ROWS, HPG * HD), bf16),
            dma((7,)),
            dma((8,)), dma((8,)), dma((8,)), dma((8,)),
            dma((8,)), dma((8,)), dma((2, 8)), dma((2,)), dma((2,)),
            dma((8,)), dma((8,)),
            dma((4,)), dma((4,)), dma((4,)), dma((4,)), dma((4,)), dma((4,)),
            dma((8,)), dma((8,)),
        ],
        compiler_params=pltpu.CompilerParams(
            collective_id=0, has_side_effects=True, vmem_limit_bytes=63 << 20
        ),
    )(queries, key_rows, value_rows, block_span, attend, noise_level, gate_table)


def solution(mesh):
    rows = P(("seq", "head"), None)
    return jax.shard_map(
        local,
        mesh=mesh,
        in_specs=(rows, rows, rows, P(), P(), P(), P()),
        out_specs=rows,
        check_vma=False,
    )
```

```python
import functools
import math

import jax
import jax.numpy as jnp
from jax import lax
from jax.experimental import pallas as pl
from jax.experimental.pallas import tpu as pltpu
from jax.sharding import PartitionSpec as P

MESH = pl.DeviceIdType.MESH
HD = 128
NX, NY, NZ = 4, 8, 8
ROWS = 16
HPG = 3
TOK = NY * ROWS
QR = HPG * TOK
COEF = HD**-0.5 * math.log2(math.e)
NEG = -1e30

Y_FAR = (4, 3, 5, 2, 6, 1, 7)
Y_NEAR = (1, 7, 2, 6, 3, 5, 4)
Z_DIRECT = (2, 6, 1, 7)
X_FAR = (2, 1, 3)


def wrap(a, n):
    return lax.rem(a + n, n)


def place():
    seq, head = lax.axis_index("seq"), lax.axis_index("head")
    z, x, y_lo = lax.rem(seq, NZ), lax.rem(seq // NZ, NX), seq // (NZ * NX)
    return x, (head // 2) * 2 + y_lo, z, lax.rem(head, 2)


def device(x, y, z, core):
    return ((lax.rem(y, 2) * NX + x) * NZ + z, (y // 2) * 2 + core)


def block_of(x, y, z):
    return ((lax.rem(y, 2) * NX + x) * NZ + z) * 2 + y // 4


def kernel(
    q_hbm, k_hbm, v_hbm, span_hbm, attend_hbm, level_hbm, gate_hbm, out_hbm,
    q_in, k_in, v_in, gate, span_ref, attend_ref, level_ref, kv, qs, kaug, qaug, acc, top, o_send, s_send, o_recv, s_recv,
    attn_send, attn, out_ref, in_sem, out_sem, ykv_s, ykv_r, yq_s, yq_r, z_s, z_r, zu_r, z4_s, z4_r, c_s, c_r, xq_s, xq_r,
    xo_s, xo_r, xs_s, xs_r, yo_s, yo_r,
):
    x, y, z, core = place()

    def at_x(d):
        return device(wrap(x + d, NX), y, z, core)

    def at_y(d):
        return device(x, wrap(y + d, NY), z, core)

    def at_z(d):
        return device(x, y, wrap(z + d, NZ), core)

    sibling = device(x, y, z, 1 - core)

    def remote(src, dst, ss, rs, to):
        return pltpu.make_async_remote_copy(
            src_ref=src, dst_ref=dst, send_sem=ss, recv_sem=rs, device_id=to, device_id_type=MESH
        )

    small = [
        pltpu.make_async_copy(span_hbm, span_ref, in_sem.at[4]),
        pltpu.make_async_copy(attend_hbm, attend_ref, in_sem.at[5]),
        pltpu.make_async_copy(level_hbm, level_ref, in_sem.at[6]),
    ]
    loads = [
        pltpu.make_async_copy(k_hbm, k_in, in_sem.at[0]),
        pltpu.make_async_copy(v_hbm, v_in, in_sem.at[1]),
        pltpu.make_async_copy(q_hbm, q_in, in_sem.at[2]),
        pltpu.make_async_copy(gate_hbm, gate, in_sem.at[3]),
    ]
    for load in small + loads:
        load.start()
    barrier = pltpu.get_barrier_semaphore()
    peers = [at_y(d) for d in Y_FAR] + [at_z(d) for d in Z_DIRECT] + [at_x(d) for d in X_FAR]
    peers.append(sibling)
    for peer in peers:
        pl.semaphore_signal(barrier, inc=1, device_id=peer, device_id_type=MESH)

    for load in small:
        load.wait()

    lane = lax.broadcasted_iota(jnp.int32, (ROWS, HD), 1)
    for i in range(NY):
        ys = wrap(y - i, NY)
        for j in range(NZ):
            span = span_ref[block_of(x, ys, wrap(z - j, NZ))]
            kaug[j, i * ROWS : (i + 1) * ROWS, :] = jnp.where(lane == span, 1.0, 0.0).astype(jnp.bfloat16)
        for j in range(NX):
            span = span_ref[block_of(wrap(x - j, NX), ys, z)]
            bias = jnp.zeros((ROWS, HD), jnp.float32)
            for s in range(4):
                low = jnp.where(attend_ref[span, s] > 0, 0.0, NEG)
                bias = jnp.where(lane == s, low, bias)
            qaug[j, i * ROWS : (i + 1) * ROWS, :] = bias.astype(jnp.bfloat16)

    for load in loads[:3]:
        load.wait()
    pl.semaphore_wait(barrier, len(peers))

    def group(d):
        return wrap(y + d, NY)

    def columns(first, count):
        return pl.ds(pl.multiple_of(first * HD, HD), count * HD)

    for d in Y_FAR:
        cols = columns(group(d), 1)
        remote(k_in.at[:, cols], kv.at[0, 0, 0, d], ykv_s.at[d], ykv_r.at[d], at_y(d)).start()
        remote(v_in.at[:, cols], kv.at[0, 0, 1, d], ykv_s.at[d], ykv_r.at[d], at_y(d)).start()
    for d in Y_FAR:
        for h in range(HPG):
            remote(
                q_in.at[:, columns(group(d) * HPG + h, 1)], qs.at[0, h, d], yq_s.at[d], yq_r.at[d], at_y(d)
            ).start()
    kv[0, 0, 0, 0] = k_in[:, columns(y, 1)]
    kv[0, 0, 1, 0] = v_in[:, columns(y, 1)]
    for h in range(HPG):
        qs[0, h, 0] = q_in[:, columns(y * HPG + h, 1)]

    def send_kv(i):
        unit = kv.at[0, 0, :, i]
        for side, d in ((0, 2), (1, 6)):
            remote(unit, kv.at[0, d, :, i], z_s.at[d], zu_r.at[side, i], at_z(d)).start()
        remote(unit, kv.at[1, 0, :, i], c_s.at[0], c_r.at[0], sibling).start()

    def send_q(i):
        for d in X_FAR:
            remote(qs.at[0, :, i], qs.at[d, :, i], xq_s.at[d], xq_r.at[d], at_x(d)).start()

    def take_kv(d):
        unit = kv.at[0, 0, :, d]
        remote(unit, unit, ykv_s.at[d], ykv_r.at[d], sibling).wait_recv()
        send_kv(d)

    def take_q(d):
        unit = qs.at[0, :, d]
        remote(unit, unit, yq_s.at[d], yq_r.at[d], sibling).wait_recv()
        send_q(d)

    def relay(i):
        for side, d, third, hop in ((0, 2, 3, 1), (1, 6, 5, 7)):
            unit, half = kv.at[0, d, :, i], kv.at[0, d, side, i]
            remote(unit, unit, z_s.at[d], zu_r.at[side, i], sibling).wait_recv()
            remote(half, kv.at[0, 4, side, i], z4_s.at[side], z4_r.at[side], at_z(d)).start()
            remote(unit, kv.at[0, third, :, i], z_s.at[third], z_r.at[third], at_z(hop)).start()
            remote(unit, kv.at[1, d, :, i], c_s.at[d], c_r.at[d], sibling).start()

    def share(d):
        remote(kv.at[0, d], kv.at[1, d], c_s.at[d], c_r.at[d], sibling).start()

    def arrive(d):
        slot = kv.at[0, d]
        remote(slot, slot, z_s.at[d], z_r.at[d], sibling).wait_recv()
        share(d)

    def from_sibling(d):
        slot = kv.at[1, d]
        remote(slot, slot, c_s.at[d], c_r.at[d], sibling).wait_recv()

    def take_block(d):
        block = qs.at[d]
        remote(block, block, xq_s.at[d], xq_r.at[d], sibling).wait_recv()

    def absorb(first, parts, groups, done=lambda b: None):
        keys = jnp.concatenate([kv[p, d, 0].reshape(TOK, HD) for p, d in parts], axis=0)
        marks = jnp.concatenate([kaug[d] for _, d in parts], axis=0)
        right = jnp.concatenate([keys, marks], axis=1)
        vals = jnp.concatenate([kv[p, d, 1].reshape(TOK, HD) for p, d in parts], axis=0)
        vals = jnp.concatenate([vals, jnp.ones(vals.shape, jnp.bfloat16)], axis=1)

        def score(group):
            left = jnp.concatenate(
                [
                    jnp.concatenate(
                        [qs[b].reshape(QR, HD), jnp.concatenate([qaug[b]] * HPG, axis=0)], axis=1
                    )
                    for b in group
                ],
                axis=0,
            )
            return lax.dot_general(left, right, (((1,), (1,)), ((), ())), preferred_element_type=jnp.float32)

        ahead = score(groups[0])
        for n, group in enumerate(groups):
            scores = ahead
            if n + 1 < len(groups) and True:
                ahead = score(groups[n + 1])
            high = jnp.max(scores, axis=1, keepdims=True)
            if first:
                old = jnp.concatenate([top[b][:, 0:1] for b in group], axis=0)
                high = jnp.maximum(high, old)
            probs = jnp.exp2((scores - high) * COEF).astype(jnp.bfloat16)
            new = jnp.dot(probs, vals, preferred_element_type=jnp.float32)
            if first:
                shrink = jnp.exp2((old - high) * COEF)
            for k, b in enumerate(group):
                rows = slice(k * QR, (k + 1) * QR)
                acc[b] = acc[b] * shrink[rows] + new[rows] if first else new[rows]
                top[b] = jnp.broadcast_to(high[rows], (QR, HD))
                done(b)
            if n + 1 < len(groups) and not True:
                ahead = score(groups[n + 1])

    near = [(0, 0), (1, 0), (0, 2), (0, 6), (1, 2), (1, 6)]
    far = [(0, 1), (0, 7), (1, 1), (1, 7), (0, 3), (0, 5), (1, 3), (1, 5), (0, 4), (1, 4)]

    send_kv(0)
    send_q(0)
    for d in (1, 7, 2, 6):
        take_kv(d)
    for d in (3, 5, 4):
        take_kv(d)
    for d in (1, 7):
        remote(kv.at[0, 0], kv.at[0, d], z_s.at[d], z_r.at[d], at_z(d)).start()
    for d in Y_NEAR:
        take_q(d)
    for d in (0,) + Y_NEAR:
        relay(d)
    arrive(1)
    arrive(7)
    for d in (0, 2, 6):
        from_sibling(d)
    take_block(1)
    take_block(3)
    take_block(2)
    absorb(0, near, [[2], [1]])
    arrive(3)
    arrive(5)
    for half in (0, 1):
        slot = kv.at[0, 4, half]
        remote(slot, slot, z4_s.at[half], z4_r.at[half], sibling).wait_recv()
        remote(slot, kv.at[1, 4, half], c_s.at[4], c_r.at[4], sibling).start()
    for d in (1, 7, 3, 5, 4):
        from_sibling(d)

    lanes = lax.broadcasted_iota(jnp.int32, (TOK, HD), 1)

    def stats_of(b):
        stats = jnp.zeros((TOK, HD), jnp.float32)
        for h in range(HPG):
            rows = slice(h * TOK, (h + 1) * TOK)
            stats = jnp.where(lanes == h, top[b, rows, :], stats)
            stats = jnp.where(lanes == HPG + h, acc[b, rows, HD : 2 * HD], stats)
        return stats.T[0:8, :]

    def give(b):
        s_send[b] = stats_of(b)
        if b:
            mean = (acc[b, :, 0:HD] / acc[b, :, HD : 2 * HD]).astype(jnp.bfloat16)
            o_send[b] = mean.reshape(HPG, NY, ROWS, HD)
            to = at_x(-b)
            remote(s_send.at[b], s_recv.at[b], xs_s.at[b], xs_r.at[b], to).start()
            for part, lo, hi in ((0, 3, 6), (1, 0, 3), (1, 6, 8)):
                remote(
                    o_send.at[b, :, lo:hi], o_recv.at[b, :, lo:hi], xo_s.at[part, b], xo_r.at[part, b], to
                ).start()

    absorb(1, far, [[2], [1]], give)
    absorb(0, near + far, [[3], [0]], give)

    for b in (1, 2, 3):
        note = s_recv.at[b]
        remote(note, note, xs_s.at[b], xs_r.at[b], sibling).wait_recv()
    notes = [s_send[0]] + [s_recv[b] for b in (1, 2, 3)]
    tops = [note[0:HPG] for note in notes]
    highest = functools.reduce(jnp.maximum, tops)
    shares = [note[HPG : 2 * HPG] * jnp.exp2((t - highest) * COEF) for note, t in zip(notes, tops)]
    whole = 1.0 / functools.reduce(jnp.add, shares)
    shares = [share_ * whole for share_ in shares]
    shares = jnp.concatenate(shares + [jnp.zeros((TOK - NX * HPG, TOK), jnp.float32)], axis=0).T

    def merge(lo, hi):
        rows = slice(lo * ROWS, hi * ROWS)
        for h in range(HPG):
            own = slice(h * TOK + lo * ROWS, h * TOK + hi * ROWS)
            total = acc[0, own, 0:HD] / acc[0, own, HD : 2 * HD] * shares[rows, h : h + 1]
            for b in (1, 2, 3):
                part = o_recv[b, h, lo:hi].reshape((hi - lo) * ROWS, HD).astype(jnp.float32)
                total = total + part * shares[rows, b * HPG + h : b * HPG + h + 1]
            total = total.astype(jnp.bfloat16).reshape(hi - lo, ROWS, HD)
            attn_send[lo:hi, :, h * HD : (h + 1) * HD] = total
        for d in range(max(lo, 1), hi):
            remote(attn_send.at[d], attn.at[y], yo_s.at[d], yo_r.at[d], at_y(-d)).start()

    for b in (1, 2, 3):
        part = o_recv.at[b, :, 3:6]
        remote(part, part, xo_s.at[0, b], xo_r.at[0, b], sibling).wait_recv()
    merge(3, 6)
    for b in (1, 2, 3):
        part = o_recv.at[b, :, 0:5]
        remote(part, part, xo_s.at[1, b], xo_r.at[1, b], sibling).wait_recv()
    merge(6, 8)
    merge(0, 3)
    attn[y] = attn_send[0]
    loads[3].wait()
    level = level_ref[span_ref[block_of(x, y, z)]]
    gates = gate[pl.ds(level, 1), :]
    for d in Y_NEAR:
        unit = attn_send.at[d]
        remote(unit, unit, yo_s.at[d], yo_r.at[d], sibling).wait_recv()
    for g in range(NY):
        cols = slice(g * HPG * HD, (g + 1) * HPG * HD)
        out_ref[:, cols] = (gates[:, cols] * attn[g].astype(jnp.float32)).astype(jnp.bfloat16)

    result = pltpu.make_async_copy(out_ref, out_hbm, out_sem)
    result.start()

    for d in Y_NEAR:
        remote(kv.at[0, 0, :, d], kv.at[0, 0, :, d], ykv_s.at[d], ykv_r.at[d], sibling).wait_send()
        remote(qs.at[0, :, d], qs.at[0, :, d], yq_s.at[d], yq_r.at[d], sibling).wait_send()
        remote(attn_send.at[d], attn_send.at[d], yo_s.at[d], yo_r.at[d], sibling).wait_send()
    for d in Z_DIRECT + (3, 5):
        remote(kv.at[0, 0], kv.at[0, 0], z_s.at[d], z_r.at[d], sibling).wait_send()
    for half in (0, 1):
        remote(kv.at[0, 4, half], kv.at[0, 4, half], z4_s.at[half], z4_r.at[half], sibling).wait_send()
    for d in range(NZ):
        remote(kv.at[0, d], kv.at[0, d], c_s.at[d], c_r.at[d], sibling).wait_send()
    for d in X_FAR:
        remote(qs.at[0], qs.at[0], xq_s.at[d], xq_r.at[d], sibling).wait_send()
        remote(o_send.at[d, :, 3:6], o_send.at[d, :, 3:6], xo_s.at[0, d], xo_r.at[0, d], sibling).wait_send()
        remote(o_send.at[d, :, 0:5], o_send.at[d, :, 0:5], xo_s.at[1, d], xo_r.at[1, d], sibling).wait_send()
        remote(s_send.at[d], s_send.at[d], xs_s.at[d], xs_r.at[d], sibling).wait_send()
    result.wait()


def local(queries, key_rows, value_rows, block_span, attend, noise_level, gate_table):
    bf16, f32 = jnp.bfloat16, jnp.float32
    dma = pltpu.SemaphoreType.DMA
    hbm = pl.BlockSpec(memory_space=pltpu.HBM)
    return pl.pallas_call(
        kernel,
        out_shape=jax.ShapeDtypeStruct(queries.shape, bf16),
        in_specs=[hbm] * 7,
        out_specs=hbm,
        scratch_shapes=[
            pltpu.VMEM(queries.shape, bf16),
            pltpu.VMEM(key_rows.shape, bf16),
            pltpu.VMEM(value_rows.shape, bf16),
            pltpu.VMEM(gate_table.shape, f32),
            pltpu.SMEM(block_span.shape, jnp.int32),
            pltpu.SMEM(attend.shape, jnp.int32),
            pltpu.SMEM(noise_level.shape, jnp.int32),
            pltpu.VMEM((2, NZ, 2, NY, ROWS, HD), bf16),
            pltpu.VMEM((NX, HPG, NY, ROWS, HD), bf16),
            pltpu.VMEM((NZ, TOK, HD), bf16),
            pltpu.VMEM((NX, TOK, HD), bf16),
            pltpu.VMEM((NX, QR, 2 * HD), f32),
            pltpu.VMEM((NX, QR, HD), f32),
            pltpu.VMEM((NX, HPG, NY, ROWS, HD), bf16),
            pltpu.VMEM((NX, 8, TOK), f32),
            pltpu.VMEM((NX, HPG, NY, ROWS, HD), bf16),
            pltpu.VMEM((NX, 8, TOK), f32),
            pltpu.VMEM((NY, ROWS, HPG * HD), bf16),
            pltpu.VMEM((NY, ROWS, HPG * HD), bf16),
            pltpu.VMEM(queries.shape, bf16),
            dma((7,)),
            dma,
            dma((8,)), dma((8,)), dma((8,)), dma((8,)),
            dma((8,)), dma((8,)), dma((2, 8)), dma((2,)), dma((2,)),
            dma((8,)), dma((8,)),
            dma((4,)), dma((4,)), dma((2, 4)), dma((2, 4)), dma((4,)), dma((4,)),
            dma((8,)), dma((8,)),
        ],
        compiler_params=pltpu.CompilerParams(
            collective_id=0, has_side_effects=True, vmem_limit_bytes=63 << 20
        ),
    )(queries, key_rows, value_rows, block_span, attend, noise_level, gate_table)


def solution(mesh):
    rows = P(("seq", "head"), None)
    return jax.shard_map(
        local,
        mesh=mesh,
        in_specs=(rows, rows, rows, P(), P(), P(), P()),
        out_specs=rows,
        check_vma=False,
    )
```

```python
import functools
import math

import jax
import jax.numpy as jnp
from jax import lax
from jax.experimental import pallas as pl
from jax.experimental.pallas import tpu as pltpu
from jax.sharding import PartitionSpec as P

MESH = pl.DeviceIdType.MESH
HD = 128
NX, NY, NZ = 4, 8, 8
ROWS = 16
HPG = 3
TOK = NY * ROWS
QR = HPG * TOK
COEF = HD**-0.5 * math.log2(math.e)
NEG = -1e30

Y_FAR = (4, 3, 5, 2, 6, 1, 7)
Y_NEAR = (1, 7, 2, 6, 3, 5, 4)
Z_DIRECT = (2, 6, 1, 7)
X_FAR = (2, 1, 3)


def wrap(a, n):
    return lax.rem(a + n, n)


def place():
    seq, head = lax.axis_index("seq"), lax.axis_index("head")
    z, x, y_lo = lax.rem(seq, NZ), lax.rem(seq // NZ, NX), seq // (NZ * NX)
    return x, (head // 2) * 2 + y_lo, z, lax.rem(head, 2)


def device(x, y, z, core):
    return ((lax.rem(y, 2) * NX + x) * NZ + z, (y // 2) * 2 + core)


def block_of(x, y, z):
    return ((lax.rem(y, 2) * NX + x) * NZ + z) * 2 + y // 4


def kernel(
    q_hbm, k_hbm, v_hbm, span_hbm, attend_hbm, level_hbm, gate_hbm, out_hbm,
    q_in, k_in, v_in, gate, span_ref, attend_ref, level_ref, kv, qs, kaug, qaug, acc, top, o_send, s_send, o_recv, s_recv,
    attn_send, attn, out_ref, in_sem, out_sem, ykv_s, ykv_r, yq_s, yq_r, z_s, z_r, zu_r, z4_s, z4_r, c_s, c_r, xq_s, xq_r,
    xo_s, xo_r, xs_s, xs_r, yo_s, yo_r,
):
    x, y, z, core = place()

    def at_x(d):
        return device(wrap(x + d, NX), y, z, core)

    def at_y(d):
        return device(x, wrap(y + d, NY), z, core)

    def at_z(d):
        return device(x, y, wrap(z + d, NZ), core)

    sibling = device(x, y, z, 1 - core)

    def remote(src, dst, ss, rs, to):
        return pltpu.make_async_remote_copy(
            src_ref=src, dst_ref=dst, send_sem=ss, recv_sem=rs, device_id=to, device_id_type=MESH
        )

    small = [
        pltpu.make_async_copy(span_hbm, span_ref, in_sem.at[4]),
        pltpu.make_async_copy(attend_hbm, attend_ref, in_sem.at[5]),
        pltpu.make_async_copy(level_hbm, level_ref, in_sem.at[6]),
    ]
    loads = [
        pltpu.make_async_copy(k_hbm, k_in, in_sem.at[0]),
        pltpu.make_async_copy(v_hbm, v_in, in_sem.at[1]),
        pltpu.make_async_copy(q_hbm, q_in, in_sem.at[2]),
        pltpu.make_async_copy(gate_hbm, gate, in_sem.at[3]),
    ]
    for load in small + loads:
        load.start()
    barrier = pltpu.get_barrier_semaphore()
    peers = [at_y(d) for d in Y_FAR] + [at_z(d) for d in Z_DIRECT] + [at_x(d) for d in X_FAR]
    peers.append(sibling)
    for peer in peers:
        pl.semaphore_signal(barrier, inc=1, device_id=peer, device_id_type=MESH)

    for load in small:
        load.wait()

    lane = lax.broadcasted_iota(jnp.int32, (ROWS, HD), 1)
    for i in range(NY):
        ys = wrap(y - i, NY)
        for j in range(NZ):
            span = span_ref[block_of(x, ys, wrap(z - j, NZ))]
            kaug[j, i * ROWS : (i + 1) * ROWS, :] = jnp.where(lane == span, 1.0, 0.0).astype(jnp.bfloat16)
        for j in range(NX):
            span = span_ref[block_of(wrap(x - j, NX), ys, z)]
            bias = jnp.zeros((ROWS, HD), jnp.float32)
            for s in range(4):
                low = jnp.where(attend_ref[span, s] > 0, 0.0, NEG)
                bias = jnp.where(lane == s, low, bias)
            qaug[j, i * ROWS : (i + 1) * ROWS, :] = bias.astype(jnp.bfloat16)

    for load in loads[:3]:
        load.wait()
    pl.semaphore_wait(barrier, len(peers))

    def group(d):
        return wrap(y + d, NY)

    def columns(first, count):
        return pl.ds(pl.multiple_of(first * HD, HD), count * HD)

    for d in Y_FAR:
        cols = columns(group(d), 1)
        remote(k_in.at[:, cols], kv.at[0, 0, 0, d], ykv_s.at[d], ykv_r.at[d], at_y(d)).start()
        remote(v_in.at[:, cols], kv.at[0, 0, 1, d], ykv_s.at[d], ykv_r.at[d], at_y(d)).start()
    for d in Y_FAR:
        for h in range(HPG):
            remote(
                q_in.at[:, columns(group(d) * HPG + h, 1)], qs.at[0, h, d], yq_s.at[d], yq_r.at[d], at_y(d)
            ).start()
    kv[0, 0, 0, 0] = k_in[:, columns(y, 1)]
    kv[0, 0, 1, 0] = v_in[:, columns(y, 1)]
    for h in range(HPG):
        qs[0, h, 0] = q_in[:, columns(y * HPG + h, 1)]

    def send_kv(i):
        unit = kv.at[0, 0, :, i]
        for side, d in ((0, 2), (1, 6)):
            remote(unit, kv.at[0, d, :, i], z_s.at[d], zu_r.at[side, i], at_z(d)).start()
        remote(unit, kv.at[1, 0, :, i], c_s.at[0], c_r.at[0], sibling).start()

    def send_q(i):
        for d in X_FAR:
            remote(qs.at[0, :, i], qs.at[d, :, i], xq_s.at[d], xq_r.at[d], at_x(d)).start()

    def take_kv(d):
        unit = kv.at[0, 0, :, d]
        remote(unit, unit, ykv_s.at[d], ykv_r.at[d], sibling).wait_recv()
        send_kv(d)

    def take_q(d):
        unit = qs.at[0, :, d]
        remote(unit, unit, yq_s.at[d], yq_r.at[d], sibling).wait_recv()
        send_q(d)

    def relay(i):
        for side, d, third, hop in ((0, 2, 3, 1), (1, 6, 5, 7)):
            unit, half = kv.at[0, d, :, i], kv.at[0, d, side, i]
            remote(unit, unit, z_s.at[d], zu_r.at[side, i], sibling).wait_recv()
            remote(half, kv.at[0, 4, side, i], z4_s.at[side], z4_r.at[side], at_z(d)).start()
            remote(unit, kv.at[0, third, :, i], z_s.at[third], z_r.at[third], at_z(hop)).start()
            remote(unit, kv.at[1, d, :, i], c_s.at[d], c_r.at[d], sibling).start()

    def share(d):
        remote(kv.at[0, d], kv.at[1, d], c_s.at[d], c_r.at[d], sibling).start()

    def arrive(d):
        slot = kv.at[0, d]
        remote(slot, slot, z_s.at[d], z_r.at[d], sibling).wait_recv()
        share(d)

    def from_sibling(d):
        slot = kv.at[1, d]
        remote(slot, slot, c_s.at[d], c_r.at[d], sibling).wait_recv()

    def take_block(d):
        block = qs.at[d]
        remote(block, block, xq_s.at[d], xq_r.at[d], sibling).wait_recv()

    def absorb(first, parts, groups, done=lambda b: None):
        keys = jnp.concatenate([kv[p, d, 0].reshape(TOK, HD) for p, d in parts], axis=0)
        marks = jnp.concatenate([kaug[d] for _, d in parts], axis=0)
        right = jnp.concatenate([keys, marks], axis=1)
        vals = jnp.concatenate([kv[p, d, 1].reshape(TOK, HD) for p, d in parts], axis=0)
        vals = jnp.concatenate([vals, jnp.ones(vals.shape, jnp.bfloat16)], axis=1)

        def score(group):
            left = jnp.concatenate(
                [
                    jnp.concatenate(
                        [qs[b].reshape(QR, HD), jnp.concatenate([qaug[b]] * HPG, axis=0)], axis=1
                    )
                    for b in group
                ],
                axis=0,
            )
            return lax.dot_general(left, right, (((1,), (1,)), ((), ())), preferred_element_type=jnp.float32)

        ahead = score(groups[0])
        for n, group in enumerate(groups):
            scores = ahead
            if n + 1 < len(groups) and True:
                ahead = score(groups[n + 1])
            high = jnp.max(scores, axis=1, keepdims=True)
            if first:
                old = jnp.concatenate([top[b][:, 0:1] for b in group], axis=0)
                high = jnp.maximum(high, old)
            probs = jnp.exp2((scores - high) * COEF).astype(jnp.bfloat16)
            new = jnp.dot(probs, vals, preferred_element_type=jnp.float32)
            if first:
                shrink = jnp.exp2((old - high) * COEF)
            for k, b in enumerate(group):
                rows = slice(k * QR, (k + 1) * QR)
                acc[b] = acc[b] * shrink[rows] + new[rows] if first else new[rows]
                top[b] = jnp.broadcast_to(high[rows], (QR, HD))
                done(b)
            if n + 1 < len(groups) and not True:
                ahead = score(groups[n + 1])

    near = [(0, 0), (1, 0), (0, 2), (0, 6), (1, 2), (1, 6)]
    far = [(0, 1), (0, 7), (1, 1), (1, 7), (0, 3), (0, 5), (1, 3), (1, 5), (0, 4), (1, 4)]

    send_kv(0)
    send_q(0)
    for d in (1, 7, 2, 6):
        take_kv(d)
    for d in (3, 5, 4):
        take_kv(d)
    for d in (1, 7):
        remote(kv.at[0, 0], kv.at[0, d], z_s.at[d], z_r.at[d], at_z(d)).start()
    relay(0)
    for d in Y_NEAR:
        take_q(d)
    for d in Y_NEAR:
        relay(d)
    arrive(1)
    arrive(7)
    for d in (0, 2, 6):
        from_sibling(d)
    take_block(2)
    take_block(1)
    absorb(0, near, [[2], [1]])
    arrive(3)
    arrive(5)
    for half in (0, 1):
        slot = kv.at[0, 4, half]
        remote(slot, slot, z4_s.at[half], z4_r.at[half], sibling).wait_recv()
        remote(slot, kv.at[1, 4, half], c_s.at[4], c_r.at[4], sibling).start()
    for d in (1, 7, 3, 5, 4):
        from_sibling(d)

    lanes = lax.broadcasted_iota(jnp.int32, (TOK, HD), 1)

    def stats_of(b):
        stats = jnp.zeros((TOK, HD), jnp.float32)
        for h in range(HPG):
            rows = slice(h * TOK, (h + 1) * TOK)
            stats = jnp.where(lanes == h, top[b, rows, :], stats)
            stats = jnp.where(lanes == HPG + h, acc[b, rows, HD : 2 * HD], stats)
        return stats.T[0:8, :]

    def give(b):
        s_send[b] = stats_of(b)
        if b:
            mean = (acc[b, :, 0:HD] / acc[b, :, HD : 2 * HD]).astype(jnp.bfloat16)
            o_send[b] = mean.reshape(HPG, NY, ROWS, HD)
            to = at_x(-b)
            remote(s_send.at[b], s_recv.at[b], xs_s.at[b], xs_r.at[b], to).start()
            for part, lo, hi in ((0, 3, 6), (1, 0, 3), (1, 6, 8)):
                remote(
                    o_send.at[b, :, lo:hi], o_recv.at[b, :, lo:hi], xo_s.at[part, b], xo_r.at[part, b], to
                ).start()

    absorb(1, far, [[2], [1]], give)
    take_block(3)
    absorb(0, near + far, [[3], [0]], give)

    for b in (1, 2, 3):
        note = s_recv.at[b]
        remote(note, note, xs_s.at[b], xs_r.at[b], sibling).wait_recv()
    notes = [s_send[0]] + [s_recv[b] for b in (1, 2, 3)]
    tops = [note[0:HPG] for note in notes]
    highest = functools.reduce(jnp.maximum, tops)
    shares = [note[HPG : 2 * HPG] * jnp.exp2((t - highest) * COEF) for note, t in zip(notes, tops)]
    whole = 1.0 / functools.reduce(jnp.add, shares)
    shares = [share_ * whole for share_ in shares]
    shares = jnp.concatenate(shares + [jnp.zeros((TOK - NX * HPG, TOK), jnp.float32)], axis=0).T

    def merge(lo, hi):
        rows = slice(lo * ROWS, hi * ROWS)
        for h in range(HPG):
            own = slice(h * TOK + lo * ROWS, h * TOK + hi * ROWS)
            total = acc[0, own, 0:HD] / acc[0, own, HD : 2 * HD] * shares[rows, h : h + 1]
            for b in (1, 2, 3):
                part = o_recv[b, h, lo:hi].reshape((hi - lo) * ROWS, HD).astype(jnp.float32)
                total = total + part * shares[rows, b * HPG + h : b * HPG + h + 1]
            total = total.astype(jnp.bfloat16).reshape(hi - lo, ROWS, HD)
            attn_send[lo:hi, :, h * HD : (h + 1) * HD] = total
        for d in range(max(lo, 1), hi):
            remote(attn_send.at[d], attn.at[y], yo_s.at[d], yo_r.at[d], at_y(-d)).start()

    for b in (1, 2, 3):
        part = o_recv.at[b, :, 3:6]
        remote(part, part, xo_s.at[0, b], xo_r.at[0, b], sibling).wait_recv()
    merge(3, 6)
    for b in (1, 2, 3):
        part = o_recv.at[b, :, 0:5]
        remote(part, part, xo_s.at[1, b], xo_r.at[1, b], sibling).wait_recv()
    merge(6, 8)
    merge(0, 3)
    attn[y] = attn_send[0]
    loads[3].wait()
    level = level_ref[span_ref[block_of(x, y, z)]]
    gates = gate[pl.ds(level, 1), :]
    for d in Y_NEAR:
        unit = attn_send.at[d]
        remote(unit, unit, yo_s.at[d], yo_r.at[d], sibling).wait_recv()
    for g in range(NY):
        cols = slice(g * HPG * HD, (g + 1) * HPG * HD)
        out_ref[:, cols] = (gates[:, cols] * attn[g].astype(jnp.float32)).astype(jnp.bfloat16)

    result = pltpu.make_async_copy(out_ref, out_hbm, out_sem)
    result.start()

    for d in Y_NEAR:
        remote(kv.at[0, 0, :, d], kv.at[0, 0, :, d], ykv_s.at[d], ykv_r.at[d], sibling).wait_send()
        remote(qs.at[0, :, d], qs.at[0, :, d], yq_s.at[d], yq_r.at[d], sibling).wait_send()
        remote(attn_send.at[d], attn_send.at[d], yo_s.at[d], yo_r.at[d], sibling).wait_send()
    for d in Z_DIRECT + (3, 5):
        remote(kv.at[0, 0], kv.at[0, 0], z_s.at[d], z_r.at[d], sibling).wait_send()
    for half in (0, 1):
        remote(kv.at[0, 4, half], kv.at[0, 4, half], z4_s.at[half], z4_r.at[half], sibling).wait_send()
    for d in range(NZ):
        remote(kv.at[0, d], kv.at[0, d], c_s.at[d], c_r.at[d], sibling).wait_send()
    for d in X_FAR:
        remote(qs.at[0], qs.at[0], xq_s.at[d], xq_r.at[d], sibling).wait_send()
        remote(o_send.at[d, :, 3:6], o_send.at[d, :, 3:6], xo_s.at[0, d], xo_r.at[0, d], sibling).wait_send()
        remote(o_send.at[d, :, 0:5], o_send.at[d, :, 0:5], xo_s.at[1, d], xo_r.at[1, d], sibling).wait_send()
        remote(s_send.at[d], s_send.at[d], xs_s.at[d], xs_r.at[d], sibling).wait_send()
    result.wait()


def local(queries, key_rows, value_rows, block_span, attend, noise_level, gate_table):
    bf16, f32 = jnp.bfloat16, jnp.float32
    dma = pltpu.SemaphoreType.DMA
    hbm = pl.BlockSpec(memory_space=pltpu.HBM)
    return pl.pallas_call(
        kernel,
        out_shape=jax.ShapeDtypeStruct(queries.shape, bf16),
        in_specs=[hbm] * 7,
        out_specs=hbm,
        scratch_shapes=[
            pltpu.VMEM(queries.shape, bf16),
            pltpu.VMEM(key_rows.shape, bf16),
            pltpu.VMEM(value_rows.shape, bf16),
            pltpu.VMEM(gate_table.shape, f32),
            pltpu.SMEM(block_span.shape, jnp.int32),
            pltpu.SMEM(attend.shape, jnp.int32),
            pltpu.SMEM(noise_level.shape, jnp.int32),
            pltpu.VMEM((2, NZ, 2, NY, ROWS, HD), bf16),
            pltpu.VMEM((NX, HPG, NY, ROWS, HD), bf16),
            pltpu.VMEM((NZ, TOK, HD), bf16),
            pltpu.VMEM((NX, TOK, HD), bf16),
            pltpu.VMEM((NX, QR, 2 * HD), f32),
            pltpu.VMEM((NX, QR, HD), f32),
            pltpu.VMEM((NX, HPG, NY, ROWS, HD), bf16),
            pltpu.VMEM((NX, 8, TOK), f32),
            pltpu.VMEM((NX, HPG, NY, ROWS, HD), bf16),
            pltpu.VMEM((NX, 8, TOK), f32),
            pltpu.VMEM((NY, ROWS, HPG * HD), bf16),
            pltpu.VMEM((NY, ROWS, HPG * HD), bf16),
            pltpu.VMEM(queries.shape, bf16),
            dma((7,)),
            dma,
            dma((8,)), dma((8,)), dma((8,)), dma((8,)),
            dma((8,)), dma((8,)), dma((2, 8)), dma((2,)), dma((2,)),
            dma((8,)), dma((8,)),
            dma((4,)), dma((4,)), dma((2, 4)), dma((2, 4)), dma((4,)), dma((4,)),
            dma((8,)), dma((8,)),
        ],
        compiler_params=pltpu.CompilerParams(
            collective_id=0, has_side_effects=True, vmem_limit_bytes=63 << 20
        ),
    )(queries, key_rows, value_rows, block_span, attend, noise_level, gate_table)


def solution(mesh):
    rows = P(("seq", "head"), None)
    return jax.shard_map(
        local,
        mesh=mesh,
        in_specs=(rows, rows, rows, P(), P(), P(), P()),
        out_specs=rows,
        check_vma=False,
    )
```
